32 devices in a mesh: bins: 8 (over y, x, core), chan: 4 (over z).
Axes of the slice: x: 2, y: 2, z: 4, core: 2. Of those that a mesh axis runs over, the one named last changes fastest.
Arguments:
- samples: float32 [8, 512, 512], P('bins', 'chan'), may hold values from -18 to 18
- groups: int32 [512], replicated, may hold values from 0 to 63, never falling along the last dimension, each value on 1 to 16 neighbouring positions
- dm_delay: int32 [2048], replicated, may hold values from 0 to 4095
- widths: int32 [8], replicated, may hold values from 0 to 4, as said below
Outputs:
- whitened: float32 [8, 512, 2048], P(None, 'bins', 'chan')
The draws below stay inside these ranges and needn't reach their ends.
Inputs may be any that keep to these rules, and one draw needn't show every extreme that they name: `groups`: group numbers never fall along the channels; each group holds 1 to 16 channels. `widths`: in every draw some band has half-width 4 and some band half-width 0.
All inputs are finite; a program needn't handle non-finite values.
Results may differ from the reference program's by a relative error of at most 0.0037.
Values may be sent and summed in bfloat16 or wider, within the bound.
A program may use at most 128 MiB of HBM per device.

```python
import math
import jax
import jax.numpy as jnp
import numpy as np
from jax import lax

CHANNELS = 512
DMS = 2048
GROUPS = 64
SAMPLES = 512
BANDS = 8
HALF = 4
DELAYMAX = 4096
PHASES = 8
TOTAL = 4096
KEEP = 4096


def draw_samples(key, part):
    noise_key, scale_key = jax.random.split(key)
    noise_draw = jnp.clip(jax.random.normal(noise_key, (PHASES, CHANNELS, SAMPLES), jnp.float32), -6.0, 6.0)
    channel_level = jnp.exp(jax.random.uniform(scale_key, (1, CHANNELS, 1), jnp.float32, math.log(0.3), math.log(3.0)))
    return noise_draw * channel_level


def draw_widths(key, part):
    first_key, second_key = jax.random.split(key)
    drawn = jax.random.randint(first_key, (BANDS,), 0, HALF + 1)
    chosen = jax.random.randint(second_key, (), 0, BANDS)
    positions = jnp.arange(BANDS)
    drawn = jnp.where(positions == chosen, HALF, drawn)
    drawn = jnp.where(positions == (chosen + 1) % BANDS, 0, drawn)
    return drawn.astype(jnp.int32)


def set_ends(values, own_key, low, top_value):
    spot = [jax.random.randint(jax.random.fold_in(own_key, axis), (), 0, length) for axis, length in enumerate(values.shape)]
    main_axis = values.shape.index(max(values.shape))
    beside = spot[:main_axis] + [(spot[main_axis] + 1) % values.shape[main_axis]] + spot[main_axis + 1:]
    return values.at[tuple(spot)].set(low).at[tuple(beside)].set(top_value)


def profile(count, total, bound, skew):
    loads = [(1 << 20) // math.isqrt(grade ** skew) + 1 for grade in range(2, count + 1)]
    spare, counts = total - bound - (count - 1), [1] * (count - 1)
    while spare > 0:
        free = [i for i in range(count - 1) if counts[i] < bound]
        whole, remaining = sum([loads[i] for i in free]), spare
        for i in free:
            extra = min(bound - counts[i], max(1, remaining * loads[i] // whole), spare)
            counts[i] = counts[i] + extra
            spare = spare - extra
    return np.array([bound] + counts)


def uneven(key, amount, total, most, lean):
    if amount == 2:
        one = jax.random.randint(key, (), max(1, total - most), min(most, total - 1) + 1)
        return jnp.stack([one, total - one])
    lengths = jnp.asarray(profile(amount, total, most, lean), jnp.int32)
    pairs = (amount - 1) // 2
    giver, sink = lengths[1:1 + 2 * pairs:2], lengths[2:2 + 2 * pairs:2]
    margin = jnp.minimum(giver - 1, most - sink)
    shifted = jax.random.randint(jax.random.fold_in(key, 1), (pairs,), 0, 1 << 20) % (margin + 1)
    lengths = lengths.at[1:1 + 2 * pairs:2].set(giver - shifted).at[2:2 + 2 * pairs:2].set(sink + shifted)
    return lengths[jax.random.permutation(jax.random.fold_in(key, 2), amount)]


def setup_inputs(seed: int = 0) -> dict:
    seeds = jax.random.split(jax.random.key(seed), 5)
    samples = draw_samples(jax.random.fold_in(seeds[4], 71), 0)
    groups = jnp.searchsorted(jnp.cumsum(uneven(seeds[1], GROUPS, CHANNELS, 2 * CHANNELS // GROUPS, 1)), jnp.arange(CHANNELS), side="right").astype(jnp.int32)
    dm_delay = set_ends(jax.random.randint(seeds[2], (DMS,), 0, DELAYMAX), jax.random.fold_in(seeds[2], 1), 0, DELAYMAX - 1).astype(jnp.int32)
    widths = draw_widths(jax.random.fold_in(seeds[4], 71), 0)
    return dict(samples=samples, groups=groups, dm_delay=dm_delay, widths=widths)


FLOOR_VALUE = 0.5


def channel_delays(dm_delay, groups):
    remain = GROUPS - groups
    sweep_scale = (2048 * remain * remain) // (GROUPS * GROUPS)
    return (dm_delay[:, None] * sweep_scale[None, :]) // 1024


def reference(samples, groups, dm_delay, widths):
    highest = lax.Precision.HIGHEST
    series = jnp.transpose(samples, (1, 2, 0)).reshape(CHANNELS, TOTAL)
    spectrum = jnp.fft.fft(series, axis=1)[:, :KEEP]
    scale_value = TOTAL ** -0.5
    real_part = (jnp.real(spectrum) * scale_value).astype(jnp.bfloat16)
    imag_part = (jnp.imag(spectrum) * scale_value).astype(jnp.bfloat16)
    delays = channel_delays(dm_delay, groups)
    angle_step = 2.0 * math.pi / TOTAL
    block_bins = 16

    def one_block(first_bin):
        bin_index = first_bin + jnp.arange(block_bins, dtype=jnp.int32)
        product = (bin_index[:, None, None] * delays[None, :, :]) % TOTAL
        phases = product.astype(jnp.float32) * angle_step
        cosine = lax.optimization_barrier(jnp.cos(phases).astype(jnp.bfloat16)).astype(jnp.float32)
        sine_part = lax.optimization_barrier(jnp.sin(phases).astype(jnp.bfloat16)).astype(jnp.float32)
        real_slice = lax.dynamic_slice_in_dim(real_part, first_bin, block_bins, 1).astype(jnp.float32)
        imag_slice = lax.dynamic_slice_in_dim(imag_part, first_bin, block_bins, 1).astype(jnp.float32)
        real_sum = jnp.einsum('bmc,cb->bm', cosine, real_slice, precision=highest) - jnp.einsum('bmc,cb->bm', sine_part, imag_slice, precision=highest)
        imag_sum = jnp.einsum('bmc,cb->bm', sine_part, real_slice, precision=highest) + jnp.einsum('bmc,cb->bm', cosine, imag_slice, precision=highest)
        return (real_sum * real_sum + imag_sum * imag_sum) / CHANNELS

    starts = jnp.arange(0, KEEP, block_bins, dtype=jnp.int32)
    powers = lax.map(one_block, starts).reshape(KEEP, DMS)
    padded = jnp.pad(powers, ((HALF, HALF), (0, 0)))
    bin_index = jnp.arange(KEEP, dtype=jnp.int32)
    half_width = jnp.repeat(widths, SAMPLES)
    window_sum = jnp.zeros((KEEP, DMS), jnp.float32)
    counted = jnp.zeros((KEEP,), jnp.float32)
    for offset in range(-HALF, HALF + 1):
        neighbour = bin_index + offset
        inside = (abs(offset) <= half_width) & (neighbour >= 0) & (neighbour < KEEP)
        weight = inside.astype(jnp.float32)
        window_sum = window_sum + weight[:, None] * padded[HALF + offset:HALF + offset + KEEP]
        counted = counted + weight
    local_mean = window_sum / counted[:, None]
    whitened = powers / jnp.maximum(local_mean, FLOOR_VALUE)
    return whitened.reshape(BANDS, SAMPLES, DMS)
```

```python
import math

import jax
import jax.numpy as jnp
import numpy as np
from jax import lax
from jax.experimental import pallas as pl
from jax.experimental.pallas import tpu as pltpu
from jax.sharding import PartitionSpec as P

CHANNELS = 512
GROUPS = 64
BANDS = 8
HALF = 4
FLOOR_VALUE = 0.5


def phasor(steps, total):
    shift = (total // 2).bit_length() - 1
    turned = steps + total // 4
    quadrant = turned >> shift
    rest = (turned & (total // 2 - 1)) - total // 4
    x = rest.astype(jnp.float32) * (math.pi / total)
    x2 = x * x
    sine = x + x * x2 * (-1 / 6 + x2 * (1 / 120 + x2 * (-1 / 5040 + x2 * (1 / 362880))))
    cosine = 1.0 + x2 * (-0.5 + x2 * (1 / 24 + x2 * (-1 / 720 + x2 * (1 / 40320))))
    odd = (quadrant & 1) == 1
    c = jnp.where(odd, sine, cosine)
    s = jnp.where(odd, cosine, sine)
    c = jnp.where(((quadrant + 1) & 2) == 2, -c, c)
    s = jnp.where((quadrant & 2) == 2, -s, s)
    return c, s


def times(a, b):
    return a[0] * b[0] - a[1] * b[1], a[0] * b[1] + a[1] * b[0]


def search(total, length, shard, scal, lhs, dm, out, centers, offset, step, powers):
    window = shard + 2 * HALF
    pairs = window // 2
    first = scal[0] * shard
    tile = dm.shape[1]
    group = lax.broadcasted_iota(jnp.int32, (GROUPS, tile), 0)
    remain = GROUPS - group
    sweep = (2048 * remain * remain) // (GROUPS * GROUPS)
    delay = (dm[...] * sweep) >> 10
    double = 2 * (first - HALF) + window - 1
    c, s = phasor(delay, total)
    offset[0], offset[1] = c, s
    c, s = phasor(2 * delay, total)
    step[0], step[1] = c, s
    wide = phasor(2 * length * delay, total)
    center = phasor(double * delay, total)
    for band in range(BANDS):
        centers[band, 0], centers[band, 1] = center
        if band < BANDS - 1:
            center = times(center, wide)

    def one_pair(j, carry):
        cb, sb = offset[0], offset[1]
        for duo in range(BANDS // 2):
            coefs = lhs[j, duo]
            high = coefs.astype(jnp.bfloat16).astype(jnp.float32)
            rows = jnp.concatenate([high, coefs - high], axis=0).astype(jnp.bfloat16)
            for part in range(2):
                band = 2 * duo + part
                ca, sa = centers[band, 0], centers[band, 1]
                table = jnp.concatenate(
                    [
                        (ca * cb).astype(jnp.bfloat16),
                        (sa * sb).astype(jnp.bfloat16),
                        (sa * cb).astype(jnp.bfloat16),
                        (ca * sb).astype(jnp.bfloat16),
                    ],
                    axis=0,
                )
                both = jnp.dot(rows, table, preferred_element_type=jnp.float32)
                value = both[:8] + both[8:]
                square = value * value
                at = 4 * part
                power = (square[at : at + 2] + square[at + 2 : at + 4]) * (1.0 / CHANNELS)
                powers[band, pl.ds(pairs + j, 1)] = power[0:1]
                powers[band, pl.ds(pairs - 1 - j, 1)] = power[1:2]
        offset[0], offset[1] = times((cb, sb), (step[0], step[1]))
        return carry

    lax.fori_loop(0, pairs, one_pair, 0)

    row = lax.broadcasted_iota(jnp.int32, (shard, tile), 0)
    for band in range(BANDS):
        half_width = scal[1 + band]
        at = row + (band * length + first)
        total_sum = jnp.zeros((shard, tile), jnp.float32)
        counted = jnp.zeros((shard, tile), jnp.float32)
        for move in range(-HALF, HALF + 1):
            near = at + move
            inside = (near >= 0) & (near < BANDS * length) & (abs(move) <= half_width)
            total_sum += jnp.where(inside, powers[band, HALF + move : HALF + move + shard], 0.0)
            counted += jnp.where(inside, 1.0, 0.0)
        middle = powers[band, HALF : HALF + shard]
        out[band] = middle / jnp.maximum(total_sum / counted, FLOOR_VALUE)


def shards(samples, groups, dm_delay, widths):
    highest = lax.Precision.HIGHEST
    phases = lax.axis_size("bins")
    chans = lax.axis_size("chan")
    phase = lax.axis_index("bins")
    chan = lax.axis_index("chan")
    local, length = samples.shape[1:]
    shard = length // phases
    total = length * phases
    window = shard + 2 * HALF
    pairs = window // 2
    share = GROUPS // chans

    mine = lax.dynamic_slice_in_dim(groups, chan * local, local)
    chosen = (mine[None, :] == jnp.arange(GROUPS, dtype=jnp.int32)[:, None]).astype(jnp.float32)
    series = jnp.dot(chosen, samples[0], precision=highest)
    series = lax.psum_scatter(series, "chan", scatter_dimension=0, tiled=True)

    bins = (np.arange(phases) * shard)[:, None] + np.arange(window)[None, :] - HALF
    turn = (np.arange(length)[:, None] * (bins.reshape(-1) % length)[None, :]) % length
    angle = turn * (2 * np.pi / length)
    scale = total**-0.5
    first = np.concatenate([np.cos(angle), -np.sin(angle)], axis=1) * scale
    freq = jnp.dot(series, jnp.asarray(first, jnp.float32), precision=highest)
    freq = freq.reshape(share, 2, phases, window)
    twist = (phase * jnp.asarray(bins, jnp.int32)).astype(jnp.float32) * (2 * math.pi / total)
    tc, ts = jnp.cos(twist), jnp.sin(twist)
    real = freq[:, 0] * tc + freq[:, 1] * ts
    imag = freq[:, 1] * tc - freq[:, 0] * ts
    blocks = jnp.stack([real, imag], axis=0).transpose(2, 0, 1, 3)
    blocks = jnp.broadcast_to(blocks[:, None], (phases, chans, 2, share, window))
    blocks = blocks.reshape(phases * chans, 2, share, window)
    got = lax.all_to_all(blocks, ("bins", "chan"), split_axis=0, concat_axis=0, tiled=True)
    got = got.reshape(phases, chans, 2, share, window)
    second = (np.arange(phases)[:, None] * np.arange(BANDS)[None, :]) % phases * (2 * np.pi / phases)
    c2, s2 = jnp.asarray(np.cos(second), jnp.float32), jnp.asarray(np.sin(second), jnp.float32)
    if phases <= 16:
        weave = lambda x, t: sum(x[i][None] * t[i][:, None, None, None] for i in range(phases))
    else:
        weave = lambda x, t: jnp.einsum("izgw,ib->bzgw", x, t, precision=highest)
    real = weave(got[:, :, 0], c2) + weave(got[:, :, 1], s2)
    imag = weave(got[:, :, 1], c2) - weave(got[:, :, 0], s2)
    real = real.reshape(BANDS, GROUPS, window)
    imag = imag.reshape(BANDS, GROUPS, window)

    rp, ip = real[:, :, pairs:], imag[:, :, pairs:]
    rm, im = real[:, :, :pairs][:, :, ::-1], imag[:, :, :pairs][:, :, ::-1]
    lhs = jnp.stack(
        [
            jnp.stack([rp, -rp, -ip, -ip]),
            jnp.stack([rm, rm, -im, im]),
            jnp.stack([ip, -ip, rp, rp]),
            jnp.stack([im, im, rm, -rm]),
        ]
    )
    lhs = lhs.transpose(4, 2, 0, 1, 3).reshape(pairs, BANDS // 2, 8, 4 * GROUPS)

    trials = dm_delay.shape[0] // chans
    tile = min(256, trials)
    dm = lax.dynamic_slice_in_dim(dm_delay, chan * trials, trials)[None, :]
    scal = jnp.concatenate([jnp.reshape(phase, (1,)), widths])
    kernel = lambda *refs: search(total, length, shard, *refs)
    return pl.pallas_call(
        kernel,
        grid=(trials // tile,),
        in_specs=[
            pl.BlockSpec(memory_space=pltpu.SMEM),
            pl.BlockSpec(lhs.shape, lambda i: (0, 0, 0, 0)),
            pl.BlockSpec((1, tile), lambda i: (0, i)),
        ],
        out_specs=pl.BlockSpec((BANDS, shard, tile), lambda i: (0, 0, i)),
        out_shape=jax.ShapeDtypeStruct((BANDS, shard, trials), jnp.float32),
        scratch_shapes=[
            pltpu.VMEM((BANDS, 2, GROUPS, tile), jnp.float32),
            pltpu.VMEM((2, GROUPS, tile), jnp.float32),
            pltpu.VMEM((2, GROUPS, tile), jnp.float32),
            pltpu.VMEM((BANDS, window, tile), jnp.float32),
        ],
        compiler_params=pltpu.CompilerParams(vmem_limit_bytes=40 * 1024 * 1024),
        cost_estimate=pl.CostEstimate(
            flops=2 * pairs * BANDS * 16 * 256 * trials, bytes_accessed=4 << 20, transcendentals=0
        ),
        name="search",
    )(scal, lhs, dm)


def solution(mesh):
    in_specs = (P("bins", "chan", None), P(), P(), P())
    out_specs = P(None, "bins", "chan")
    return jax.shard_map(shards, mesh=mesh, in_specs=in_specs, out_specs=out_specs, check_vma=False)
```

```python
import math

import jax
import jax.numpy as jnp
import numpy as np
from jax import lax
from jax.experimental import pallas as pl
from jax.experimental.pallas import tpu as pltpu
from jax.sharding import PartitionSpec as P

CHANNELS = 512
GROUPS = 64
BANDS = 8
HALF = 4
FLOOR_VALUE = 0.5
TILE = 256
MESH = pl.DeviceIdType.MESH


def phasor(steps, total):
    shift = (total // 2).bit_length() - 1
    turned = steps + total // 4
    quadrant = turned >> shift
    rest = (turned & (total // 2 - 1)) - total // 4
    x = rest.astype(jnp.float32) * (math.pi / total)
    x2 = x * x
    sine = x + x * x2 * (-1 / 6 + x2 * (1 / 120 + x2 * (-1 / 5040 + x2 * (1 / 362880))))
    cosine = 1.0 + x2 * (-0.5 + x2 * (1 / 24 + x2 * (-1 / 720 + x2 * (1 / 40320))))
    odd = (quadrant & 1) == 1
    c = jnp.where(odd, sine, cosine)
    s = jnp.where(odd, cosine, sine)
    c = jnp.where(((quadrant + 1) & 2) == 2, -c, c)
    s = jnp.where((quadrant & 2) == 2, -s, s)
    return c, s


def times(a, b):
    return a[0] * b[0] - a[1] * b[1], a[0] * b[1] + a[1] * b[0]


def front(phases, chans, shard, samples, groups, table_hbm, out, table, parts, gathered, near, blocks, arrived,
          load_sem, send_sem, recv_sem):
    phase, chan = lax.axis_index("bins"), lax.axis_index("chan")
    window = shard + 2 * HALF
    total = phases * samples.shape[2]
    share = GROUPS // chans
    load = pltpu.make_async_copy(table_hbm, table, load_sem)
    load.start()
    barrier = pltpu.get_barrier_semaphore()
    for off in range(1, chans):
        pl.semaphore_signal(barrier, 1, device_id=(phase, lax.rem(chan + off, chans)), device_id_type=MESH)
    for off in range(1, phases):
        pl.semaphore_signal(barrier, 1, device_id=(lax.rem(phase + off, phases), chan), device_id_type=MESH)

    mine = groups[pl.ds(chan, 1), :]
    chosen = jnp.where(
        mine == lax.broadcasted_iota(jnp.int32, (GROUPS, groups.shape[1]), 0), 1.0, 0.0
    )
    series = jnp.dot(
        chosen, samples[0], precision=lax.Precision.HIGHEST, preferred_element_type=jnp.float32
    )
    parts[...] = series.reshape(parts.shape)
    pl.semaphore_wait(barrier, chans + phases - 2)

    copies = []
    for off in range(1, chans):
        peer = lax.rem(chan + off, chans)
        copy = pltpu.make_async_remote_copy(
            src_ref=parts.at[peer],
            dst_ref=near.at[off - 1],
            send_sem=send_sem.at[off - 1],
            recv_sem=recv_sem.at[off - 1],
            device_id=(phase, peer),
            device_id_type=MESH,
        )
        copy.start()
        copies.append(copy)
    shape = (phases, window, GROUPS)
    place = lax.broadcasted_iota(jnp.int32, shape, 0) * shard + lax.broadcasted_iota(jnp.int32, shape, 1) - HALF
    tc, ts = phasor((2 * phase * place) & (2 * total - 1), total)
    own = parts[chan]
    for copy in copies:
        copy.wait()
    for off in range(1, chans):
        own = own + near[off - 1]
    gathered[pl.ds(chan, 1)] = own[None]

    copies = []
    for off in range(1, chans):
        copy = pltpu.make_async_remote_copy(
            src_ref=gathered.at[chan],
            dst_ref=gathered.at[chan],
            send_sem=send_sem.at[chans - 2 + off],
            recv_sem=recv_sem.at[chans - 2 + off],
            device_id=(phase, lax.rem(chan + off, chans)),
            device_id_type=MESH,
        )
        copy.start()
        copies.append(copy)
    load.wait()
    for copy in copies:
        copy.wait()

    whole = gathered[...].reshape(GROUPS, samples.shape[2])
    high = whole.astype(jnp.bfloat16)
    low = (whole - high.astype(jnp.float32)).astype(jnp.bfloat16)
    dims = (((1,), (1,)), ((), ()))
    freq = (
        lax.dot_general(table[0], high, dims, preferred_element_type=jnp.float32)
        + lax.dot_general(table[0], low, dims, preferred_element_type=jnp.float32)
        + lax.dot_general(table[1], high, dims, preferred_element_type=jnp.float32)
    )
    real = freq[: phases * window].reshape(shape)
    imag = freq[phases * window :].reshape(shape)
    blocks[...] = jnp.concatenate([real * tc + imag * ts, imag * tc - real * ts], axis=2)
    copies = []
    for off in range(1, phases):
        peer = lax.rem(phase + off, phases)
        slot = 2 * (chans - 1) + off - 1
        copy = pltpu.make_async_remote_copy(
            src_ref=blocks.at[peer],
            dst_ref=arrived.at[phase],
            send_sem=send_sem.at[slot],
            recv_sem=recv_sem.at[slot],
            device_id=(peer, chan),
            device_id_type=MESH,
        )
        copy.start()
        copies.append(copy)
    arrived[pl.ds(phase, 1)] = blocks[pl.ds(phase, 1)]
    for copy in copies:
        copy.wait()
    lane = lax.broadcasted_iota(jnp.int32, (window, 2 * GROUPS), 1)
    sign = jnp.where(lane < GROUPS, 1.0, -1.0)
    for band in range(BANDS):
        straight = jnp.zeros((window, 2 * GROUPS), jnp.float32)
        crossed = jnp.zeros((window, 2 * GROUPS), jnp.float32)
        for source in range(phases):
            angle = 2 * math.pi * (source * band % phases) / phases
            block = arrived[source]
            straight += block * math.cos(angle)
            crossed += block * math.sin(angle)
        out[band] = straight + pltpu.roll(crossed, GROUPS, 1) * sign


def search(total, length, shard, widths, spectra, dm, out, centers, offset, step, powers):
    window = shard + 2 * HALF
    pairs = window // 2
    first = lax.axis_index("bins") * shard
    tile = dm.shape[1]
    group = lax.broadcasted_iota(jnp.int32, (GROUPS, tile), 0)
    remain = GROUPS - group
    sweep = (2048 * remain * remain) // (GROUPS * GROUPS)
    delay = (dm[pl.ds(lax.axis_index("chan"), 1), :] * sweep) >> 10
    double = 2 * (first - HALF) + window - 1
    c, s = phasor(delay, total)
    offset[0], offset[1] = c, s
    c, s = phasor(2 * delay, total)
    step[0], step[1] = c, s
    wide = phasor(2 * length * delay, total)
    center = phasor(double * delay, total)
    for band in range(BANDS):
        centers[band, 0], centers[band, 1] = center
        if band < BANDS - 1:
            center = times(center, wide)

    tile8 = (8, 2 * GROUPS)
    row8 = lax.broadcasted_iota(jnp.int32, tile8, 0)
    left = lax.broadcasted_iota(jnp.int32, tile8, 1) < GROUPS
    real_row = (row8 & 1) == 0
    plus_row = (row8 & 2) == 0
    low_part = row8 < 4
    sign_first = jnp.where(real_row & ~left, -1.0, 1.0)
    sign_second = jnp.where(plus_row & (real_row | left) | ~plus_row & ~real_row & ~left, -1.0, 1.0)

    def one_pair(j, carry):
        cb, sb = offset[0], offset[1]
        for duo in range(BANDS // 2):
            row = [
                jnp.broadcast_to(spectra[2 * duo + part, pl.ds(at, 1), :], tile8)
                for part in range(2)
                for at in (pairs + j, pairs - 1 - j)
            ]
            value = jnp.where(
                low_part, jnp.where(plus_row, row[0], row[1]), jnp.where(plus_row, row[2], row[3])
            )
            value = jnp.where(real_row, value, pltpu.roll(value, GROUPS, 1))
            coefs = jnp.concatenate([value * sign_first, value * sign_second], axis=1)
            high = coefs.astype(jnp.bfloat16).astype(jnp.float32)
            rows = jnp.concatenate([high, coefs - high], axis=0).astype(jnp.bfloat16)
            for part in range(2):
                band = 2 * duo + part
                ca, sa = centers[band, 0], centers[band, 1]
                table = jnp.concatenate(
                    [
                        (ca * cb).astype(jnp.bfloat16),
                        (sa * cb).astype(jnp.bfloat16),
                        (sa * sb).astype(jnp.bfloat16),
                        (ca * sb).astype(jnp.bfloat16),
                    ],
                    axis=0,
                )
                both = jnp.dot(rows, table, preferred_element_type=jnp.float32)
                total_rows = both[:8] + both[8:]
                square = total_rows * total_rows * (1.0 / CHANNELS)
                at = 4 * part
                powers[band, pl.ds(pairs + j, 1)] = square[at : at + 1] + square[at + 1 : at + 2]
                powers[band, pl.ds(pairs - 1 - j, 1)] = square[at + 2 : at + 3] + square[at + 3 : at + 4]
        offset[0], offset[1] = times((cb, sb), (step[0], step[1]))
        return carry

    lax.fori_loop(0, pairs, one_pair, 0)

    row = lax.broadcasted_iota(jnp.int32, (shard, tile), 0)
    for band in range(BANDS):
        half_width = widths[band]
        at = row + (band * length + first)
        total_sum = jnp.zeros((shard, tile), jnp.float32)
        counted = jnp.zeros((shard, tile), jnp.float32)
        for move in range(-HALF, HALF + 1):
            near = at + move
            inside = (near >= 0) & (near < BANDS * length) & (abs(move) <= half_width)
            total_sum += jnp.where(inside, powers[band, HALF + move : HALF + move + shard], 0.0)
            counted += jnp.where(inside, 1.0, 0.0)
        middle = powers[band, HALF : HALF + shard]
        out[band] = middle / jnp.maximum(total_sum / counted, FLOOR_VALUE)


def block_bins(phases, shard):
    return (np.arange(phases) * shard)[:, None] + np.arange(shard + 2 * HALF)[None, :] - HALF


def spectra_by_kernel(samples, groups, phases, chans, shard):
    local, length = samples.shape[1:]
    window = shard + 2 * HALF
    bins = block_bins(phases, shard)
    turn = ((bins.reshape(-1) % length)[:, None] * np.arange(length)[None, :]) % length
    angle = turn * (2 * np.pi / length)
    scale = (length * phases) ** -0.5
    exact = (np.concatenate([np.cos(angle), -np.sin(angle)], axis=0) * scale).astype(np.float32)
    high = exact.astype(jnp.bfloat16)
    low = (exact - high.astype(np.float32)).astype(jnp.bfloat16)
    table = jnp.asarray(np.stack([high, low]))
    share = GROUPS // chans
    copies = 2 * (chans - 1) + phases - 1
    vmem = pl.BlockSpec(memory_space=pltpu.VMEM)
    return pl.pallas_call(
        lambda *refs: front(phases, chans, shard, *refs),
        in_specs=[vmem, vmem, pl.BlockSpec(memory_space=pl.ANY)],
        out_specs=vmem,
        out_shape=jax.ShapeDtypeStruct((BANDS, window, 2 * GROUPS), jnp.float32),
        scratch_shapes=[
            pltpu.VMEM(table.shape, jnp.bfloat16),
            pltpu.VMEM((chans, share, length), jnp.float32),
            pltpu.VMEM((chans, share, length), jnp.float32),
            pltpu.VMEM((chans - 1, share, length), jnp.float32),
            pltpu.VMEM((phases, window, 2 * GROUPS), jnp.float32),
            pltpu.VMEM((phases, window, 2 * GROUPS), jnp.float32),
            pltpu.SemaphoreType.DMA,
            pltpu.SemaphoreType.DMA((copies,)),
            pltpu.SemaphoreType.DMA((copies,)),
        ],
        compiler_params=pltpu.CompilerParams(
            collective_id=0, has_side_effects=True, vmem_limit_bytes=32 * 1024 * 1024
        ),
        cost_estimate=pl.CostEstimate(flops=1 << 28, bytes_accessed=4 << 20, transcendentals=0),
        name="front",
    )(samples, groups.reshape(chans, local), table)


def spectra_by_collectives(samples, groups, phases, chans, shard):
    highest = lax.Precision.HIGHEST
    phase = lax.axis_index("bins")
    chan = lax.axis_index("chan")
    local, length = samples.shape[1:]
    total = length * phases
    window = shard + 2 * HALF
    share = GROUPS // chans
    mine = lax.dynamic_slice_in_dim(groups, chan * local, local)
    chosen = (mine[None, :] == jnp.arange(GROUPS, dtype=jnp.int32)[:, None]).astype(jnp.float32)
    series = jnp.dot(chosen, samples[0], precision=highest)
    series = lax.psum_scatter(series, "chan", scatter_dimension=0, tiled=True)

    bins = block_bins(phases, shard)
    turn = (np.arange(length)[:, None] * (bins.reshape(-1) % length)[None, :]) % length
    angle = turn * (2 * np.pi / length)
    scale = total**-0.5
    first = np.concatenate([np.cos(angle), -np.sin(angle)], axis=1) * scale
    freq = jnp.dot(series, jnp.asarray(first, jnp.float32), precision=highest)
    freq = freq.reshape(share, 2, phases, window)
    twist = (phase * jnp.asarray(bins, jnp.int32)).astype(jnp.float32) * (2 * math.pi / total)
    tc, ts = jnp.cos(twist), jnp.sin(twist)
    real = freq[:, 0] * tc + freq[:, 1] * ts
    imag = freq[:, 1] * tc - freq[:, 0] * ts
    blocks = jnp.stack([real, imag], axis=0).transpose(2, 0, 1, 3)
    blocks = jnp.broadcast_to(blocks[:, None], (phases, chans, 2, share, window))
    blocks = blocks.reshape(phases * chans, 2, share, window)
    got = lax.all_to_all(blocks, ("bins", "chan"), split_axis=0, concat_axis=0, tiled=True)
    got = got.reshape(phases, chans, 2, share, window)
    second = (np.arange(phases)[:, None] * np.arange(BANDS)[None, :]) % phases * (2 * np.pi / phases)
    c2, s2 = jnp.asarray(np.cos(second), jnp.float32), jnp.asarray(np.sin(second), jnp.float32)
    weave = lambda x, t: jnp.einsum("izgw,ib->bwzg", x, t, precision=highest)
    real = weave(got[:, :, 0], c2) + weave(got[:, :, 1], s2)
    imag = weave(got[:, :, 1], c2) - weave(got[:, :, 0], s2)
    return jnp.stack([real, imag], axis=2).reshape(BANDS, window, 2 * GROUPS)


def shards(samples, groups, dm_delay, widths):
    phases = lax.axis_size("bins")
    chans = lax.axis_size("chan")
    length = samples.shape[2]
    shard = length // phases
    total = length * phases
    window = shard + 2 * HALF
    pairs = window // 2
    make = spectra_by_kernel if window % 8 == 0 else spectra_by_collectives
    spectra = make(samples, groups, phases, chans, shard)
    trials = dm_delay.shape[0] // chans
    tile = min(TILE, trials)
    return pl.pallas_call(
        lambda *refs: search(total, length, shard, *refs),
        grid=(trials // tile,),
        in_specs=[
            pl.BlockSpec(memory_space=pltpu.SMEM),
            pl.BlockSpec(spectra.shape, lambda i: (0, 0, 0)),
            pl.BlockSpec((chans, tile), lambda i: (0, i)),
        ],
        out_specs=pl.BlockSpec((BANDS, shard, tile), lambda i: (0, 0, i)),
        out_shape=jax.ShapeDtypeStruct((BANDS, shard, trials), jnp.float32),
        scratch_shapes=[
            pltpu.VMEM((BANDS, 2, GROUPS, tile), jnp.float32),
            pltpu.VMEM((2, GROUPS, tile), jnp.float32),
            pltpu.VMEM((2, GROUPS, tile), jnp.float32),
            pltpu.VMEM((BANDS, window, tile), jnp.float32),
        ],
        compiler_params=pltpu.CompilerParams(vmem_limit_bytes=40 * 1024 * 1024),
        cost_estimate=pl.CostEstimate(
            flops=2 * pairs * BANDS * 16 * 256 * trials, bytes_accessed=4 << 20, transcendentals=0
        ),
        name="search",
    )(widths, spectra, dm_delay.reshape(chans, trials))


def solution(mesh):
    in_specs = (P("bins", "chan", None), P(), P(), P())
    out_specs = P(None, "bins", "chan")
    return jax.shard_map(shards, mesh=mesh, in_specs=in_specs, out_specs=out_specs, check_vma=False)
```

```python
import math

import jax
import jax.numpy as jnp
import numpy as np
from jax import lax
from jax.experimental import pallas as pl
from jax.experimental.pallas import tpu as pltpu
from jax.sharding import PartitionSpec as P

CHANNELS = 512
GROUPS = 64
BANDS = 8
HALF = 4
FLOOR_VALUE = 0.5
TILE = 512
MESH = pl.DeviceIdType.MESH


def phasor(steps, total):
    shift = (total // 2).bit_length() - 1
    turned = steps + total // 4
    quadrant = turned >> shift
    rest = (turned & (total // 2 - 1)) - total // 4
    x = rest.astype(jnp.float32) * (math.pi / total)
    x2 = x * x
    sine = x + x * x2 * (-1 / 6 + x2 * (1 / 120 + x2 * (-1 / 5040 + x2 * (1 / 362880))))
    cosine = 1.0 + x2 * (-0.5 + x2 * (1 / 24 + x2 * (-1 / 720 + x2 * (1 / 40320))))
    odd = (quadrant & 1) == 1
    c = jnp.where(odd, sine, cosine)
    s = jnp.where(odd, cosine, sine)
    c = jnp.where(((quadrant + 1) & 2) == 2, -c, c)
    s = jnp.where((quadrant & 2) == 2, -s, s)
    return c, s


def times(a, b):
    return a[0] * b[0] - a[1] * b[1], a[0] * b[1] + a[1] * b[0]


def front(phases, chans, shard, samples, groups, table_hbm, out, table, parts, gathered, near, blocks, arrived,
          load_sem, send_sem, recv_sem):
    phase, chan = lax.axis_index("bins"), lax.axis_index("chan")
    window = shard + 2 * HALF
    total = phases * samples.shape[2]
    share = GROUPS // chans
    load = pltpu.make_async_copy(table_hbm, table, load_sem)
    load.start()
    barrier = pltpu.get_barrier_semaphore()
    for off in range(1, chans):
        pl.semaphore_signal(barrier, 1, device_id=(phase, lax.rem(chan + off, chans)), device_id_type=MESH)
    for off in range(1, phases):
        pl.semaphore_signal(barrier, 1, device_id=(lax.rem(phase + off, phases), chan), device_id_type=MESH)

    mine = groups[pl.ds(chan, 1), :]
    chosen = jnp.where(
        mine == lax.broadcasted_iota(jnp.int32, (GROUPS, groups.shape[1]), 0), 1.0, 0.0
    )
    series = jnp.dot(
        chosen, samples[0], precision=lax.Precision.HIGHEST, preferred_element_type=jnp.float32
    )
    parts[...] = series.reshape(parts.shape)
    pl.semaphore_wait(barrier, chans + phases - 2)

    copies = []
    for off in range(1, chans):
        peer = lax.rem(chan + off, chans)
        copy = pltpu.make_async_remote_copy(
            src_ref=parts.at[peer],
            dst_ref=near.at[off - 1],
            send_sem=send_sem.at[off - 1],
            recv_sem=recv_sem.at[off - 1],
            device_id=(phase, peer),
            device_id_type=MESH,
        )
        copy.start()
        copies.append(copy)
    shape = (phases, window, GROUPS)
    place = lax.broadcasted_iota(jnp.int32, shape, 0) * shard + lax.broadcasted_iota(jnp.int32, shape, 1) - HALF
    tc, ts = phasor((2 * phase * place) & (2 * total - 1), total)
    own = parts[chan]
    for copy in copies:
        copy.wait()
    for off in range(1, chans):
        own = own + near[off - 1]
    gathered[pl.ds(chan, 1)] = own[None]

    copies = []
    for off in range(1, chans):
        copy = pltpu.make_async_remote_copy(
            src_ref=gathered.at[chan],
            dst_ref=gathered.at[chan],
            send_sem=send_sem.at[chans - 2 + off],
            recv_sem=recv_sem.at[chans - 2 + off],
            device_id=(phase, lax.rem(chan + off, chans)),
            device_id_type=MESH,
        )
        copy.start()
        copies.append(copy)
    load.wait()
    for copy in copies:
        copy.wait()

    whole = gathered[...].reshape(GROUPS, samples.shape[2])
    high = whole.astype(jnp.bfloat16)
    low = (whole - high.astype(jnp.float32)).astype(jnp.bfloat16)
    dims = (((1,), (1,)), ((), ()))
    freq = (
        lax.dot_general(table[0], high, dims, preferred_element_type=jnp.float32)
        + lax.dot_general(table[0], low, dims, preferred_element_type=jnp.float32)
        + lax.dot_general(table[1], high, dims, preferred_element_type=jnp.float32)
    )
    real = freq[: phases * window].reshape(shape)
    imag = freq[phases * window :].reshape(shape)
    blocks[...] = jnp.concatenate([real * tc + imag * ts, imag * tc - real * ts], axis=2)
    copies = []
    for off in range(1, phases):
        peer = lax.rem(phase + off, phases)
        slot = 2 * (chans - 1) + off - 1
        copy = pltpu.make_async_remote_copy(
            src_ref=blocks.at[peer],
            dst_ref=arrived.at[phase],
            send_sem=send_sem.at[slot],
            recv_sem=recv_sem.at[slot],
            device_id=(peer, chan),
            device_id_type=MESH,
        )
        copy.start()
        copies.append(copy)
    arrived[pl.ds(phase, 1)] = blocks[pl.ds(phase, 1)]
    for copy in copies:
        copy.wait()
    lane = lax.broadcasted_iota(jnp.int32, (window, 2 * GROUPS), 1)
    sign = jnp.where(lane < GROUPS, 1.0, -1.0)
    for band in range(BANDS):
        straight = jnp.zeros((window, 2 * GROUPS), jnp.float32)
        crossed = jnp.zeros((window, 2 * GROUPS), jnp.float32)
        for source in range(phases):
            angle = 2 * math.pi * (source * band % phases) / phases
            block = arrived[source]
            straight += block * math.cos(angle)
            crossed += block * math.sin(angle)
        out[band] = straight + pltpu.roll(crossed, GROUPS, 1) * sign


def search(total, length, shard, widths, spectra, dm, out, centers, offset, step, powers):
    window = shard + 2 * HALF
    pairs = window // 2
    first = lax.axis_index("bins") * shard
    tile = dm.shape[1]
    group = lax.broadcasted_iota(jnp.int32, (GROUPS, tile), 0)
    remain = GROUPS - group
    sweep = (2048 * remain * remain) // (GROUPS * GROUPS)
    delay = (dm[pl.ds(lax.axis_index("chan"), 1), :] * sweep) >> 10
    double = 2 * (first - HALF) + window - 1
    c, s = phasor(delay, total)
    offset[0], offset[1] = c, s
    c, s = phasor(2 * delay, total)
    step[0], step[1] = c, s
    wide = phasor(2 * length * delay, total)
    center = phasor(double * delay, total)
    for band in range(BANDS):
        centers[band, 0], centers[band, 1] = center
        if band < BANDS - 1:
            center = times(center, wide)

    tile8 = (8, 2 * GROUPS)
    row8 = lax.broadcasted_iota(jnp.int32, tile8, 0)
    left = lax.broadcasted_iota(jnp.int32, tile8, 1) < GROUPS
    real_row = (row8 & 1) == 0
    plus_row = (row8 & 2) == 0
    low_part = row8 < 4
    sign_first = jnp.where(real_row & ~left, -1.0, 1.0)
    sign_second = jnp.where(plus_row & (real_row | left) | ~plus_row & ~real_row & ~left, -1.0, 1.0)

    def one_pair(j, carry):
        cb, sb = offset[0], offset[1]
        for duo in range(BANDS // 2):
            row = [
                jnp.broadcast_to(spectra[2 * duo + part, pl.ds(at, 1), :], tile8)
                for part in range(2)
                for at in (pairs + j, pairs - 1 - j)
            ]
            value = jnp.where(
                low_part, jnp.where(plus_row, row[0], row[1]), jnp.where(plus_row, row[2], row[3])
            )
            value = jnp.where(real_row, value, pltpu.roll(value, GROUPS, 1))
            coefs = jnp.concatenate([value * sign_first, value * sign_second], axis=1)
            high = coefs.astype(jnp.bfloat16).astype(jnp.float32)
            rows = jnp.concatenate([high, coefs - high], axis=0).astype(jnp.bfloat16)
            for part in range(2):
                band = 2 * duo + part
                ca, sa = centers[band, 0], centers[band, 1]
                table = jnp.concatenate(
                    [
                        (ca * cb).astype(jnp.bfloat16),
                        (sa * cb).astype(jnp.bfloat16),
                        (sa * sb).astype(jnp.bfloat16),
                        (ca * sb).astype(jnp.bfloat16),
                    ],
                    axis=0,
                )
                both = jnp.dot(rows, table, preferred_element_type=jnp.float32)
                total_rows = both[:8] + both[8:]
                square = total_rows * total_rows * (1.0 / CHANNELS)
                at = 4 * part
                powers[band, pl.ds(pairs + j, 1)] = square[at : at + 1] + square[at + 1 : at + 2]
                powers[band, pl.ds(pairs - 1 - j, 1)] = square[at + 2 : at + 3] + square[at + 3 : at + 4]
        offset[0], offset[1] = times((cb, sb), (step[0], step[1]))
        return carry

    lax.fori_loop(0, pairs, one_pair, 0)

    @pl.when(first == 0)
    def _():
        powers[0, 0:HALF] = jnp.zeros((HALF, tile), jnp.float32)

    @pl.when(first + shard == length)
    def _():
        powers[BANDS - 1, HALF + shard : window] = jnp.zeros((HALF, tile), jnp.float32)

    row = lax.broadcasted_iota(jnp.int32, (shard, 128), 0)
    for band in range(BANDS):
        half_width = widths[band]
        at = row + (band * length + first)
        low_end = jnp.maximum(at - half_width, 0)
        high_end = jnp.minimum(at + half_width, BANDS * length - 1)
        part = 1.0 / (high_end - low_end + 1).astype(jnp.float32)
        weight = [jnp.where(move <= half_width, 1.0, 0.0) for move in range(HALF + 1)]
        for column in range(0, tile, 128):
            lanes = slice(column, column + 128)
            middle = powers[band, HALF : HALF + shard, lanes]
            total_sum = middle
            for move in range(1, HALF + 1):
                total_sum += weight[move] * (
                    powers[band, HALF - move : HALF - move + shard, lanes]
                    + powers[band, HALF + move : HALF + move + shard, lanes]
                )
            out[band, :, lanes] = middle / jnp.maximum(total_sum * part, FLOOR_VALUE)


def block_bins(phases, shard):
    return (np.arange(phases) * shard)[:, None] + np.arange(shard + 2 * HALF)[None, :] - HALF


def spectra_by_kernel(samples, groups, phases, chans, shard):
    local, length = samples.shape[1:]
    window = shard + 2 * HALF
    bins = block_bins(phases, shard)
    turn = ((bins.reshape(-1) % length)[:, None] * np.arange(length)[None, :]) % length
    angle = turn * (2 * np.pi / length)
    scale = (length * phases) ** -0.5
    exact = (np.concatenate([np.cos(angle), -np.sin(angle)], axis=0) * scale).astype(np.float32)
    high = exact.astype(jnp.bfloat16)
    low = (exact - high.astype(np.float32)).astype(jnp.bfloat16)
    table = jnp.asarray(np.stack([high, low]))
    share = GROUPS // chans
    copies = 2 * (chans - 1) + phases - 1
    vmem = pl.BlockSpec(memory_space=pltpu.VMEM)
    return pl.pallas_call(
        lambda *refs: front(phases, chans, shard, *refs),
        in_specs=[vmem, vmem, pl.BlockSpec(memory_space=pl.ANY)],
        out_specs=vmem,
        out_shape=jax.ShapeDtypeStruct((BANDS, window, 2 * GROUPS), jnp.float32),
        scratch_shapes=[
            pltpu.VMEM(table.shape, jnp.bfloat16),
            pltpu.VMEM((chans, share, length), jnp.float32),
            pltpu.VMEM((chans, share, length), jnp.float32),
            pltpu.VMEM((chans - 1, share, length), jnp.float32),
            pltpu.VMEM((phases, window, 2 * GROUPS), jnp.float32),
            pltpu.VMEM((phases, window, 2 * GROUPS), jnp.float32),
            pltpu.SemaphoreType.DMA,
            pltpu.SemaphoreType.DMA((copies,)),
            pltpu.SemaphoreType.DMA((copies,)),
        ],
        compiler_params=pltpu.CompilerParams(
            collective_id=0, has_side_effects=True, vmem_limit_bytes=60 * 1024 * 1024
        ),
        cost_estimate=pl.CostEstimate(flops=1 << 28, bytes_accessed=4 << 20, transcendentals=0),
        name="front",
    )(samples, groups.reshape(chans, local), table)


def spectra_by_collectives(samples, groups, phases, chans, shard):
    highest = lax.Precision.HIGHEST
    phase = lax.axis_index("bins")
    chan = lax.axis_index("chan")
    local, length = samples.shape[1:]
    total = length * phases
    window = shard + 2 * HALF
    share = GROUPS // chans
    mine = lax.dynamic_slice_in_dim(groups, chan * local, local)
    chosen = (mine[None, :] == jnp.arange(GROUPS, dtype=jnp.int32)[:, None]).astype(jnp.float32)
    series = jnp.dot(chosen, samples[0], precision=highest)
    series = lax.psum_scatter(series, "chan", scatter_dimension=0, tiled=True)

    bins = block_bins(phases, shard)
    turn = (np.arange(length)[:, None] * (bins.reshape(-1) % length)[None, :]) % length
    angle = turn * (2 * np.pi / length)
    scale = total**-0.5
    first = np.concatenate([np.cos(angle), -np.sin(angle)], axis=1) * scale
    freq = jnp.dot(series, jnp.asarray(first, jnp.float32), precision=highest)
    freq = freq.reshape(share, 2, phases, window)
    twist = (phase * jnp.asarray(bins, jnp.int32)).astype(jnp.float32) * (2 * math.pi / total)
    tc, ts = jnp.cos(twist), jnp.sin(twist)
    real = freq[:, 0] * tc + freq[:, 1] * ts
    imag = freq[:, 1] * tc - freq[:, 0] * ts
    blocks = jnp.stack([real, imag], axis=0).transpose(2, 0, 1, 3)
    blocks = jnp.broadcast_to(blocks[:, None], (phases, chans, 2, share, window))
    blocks = blocks.reshape(phases * chans, 2, share, window)
    got = lax.all_to_all(blocks, ("bins", "chan"), split_axis=0, concat_axis=0, tiled=True)
    got = got.reshape(phases, chans, 2, share, window)
    second = (np.arange(phases)[:, None] * np.arange(BANDS)[None, :]) % phases * (2 * np.pi / phases)
    c2, s2 = jnp.asarray(np.cos(second), jnp.float32), jnp.asarray(np.sin(second), jnp.float32)
    weave = lambda x, t: jnp.einsum("izgw,ib->bwzg", x, t, precision=highest)
    real = weave(got[:, :, 0], c2) + weave(got[:, :, 1], s2)
    imag = weave(got[:, :, 1], c2) - weave(got[:, :, 0], s2)
    return jnp.stack([real, imag], axis=2).reshape(BANDS, window, 2 * GROUPS)


def shards(samples, groups, dm_delay, widths):
    phases = lax.axis_size("bins")
    chans = lax.axis_size("chan")
    length = samples.shape[2]
    shard = length // phases
    total = length * phases
    window = shard + 2 * HALF
    pairs = window // 2
    make = spectra_by_kernel if window % 8 == 0 else spectra_by_collectives
    spectra = make(samples, groups, phases, chans, shard)
    trials = dm_delay.shape[0] // chans
    tile = min(TILE, trials)
    return pl.pallas_call(
        lambda *refs: search(total, length, shard, *refs),
        grid=(trials // tile,),
        in_specs=[
            pl.BlockSpec(memory_space=pltpu.SMEM),
            pl.BlockSpec(spectra.shape, lambda i: (0, 0, 0)),
            pl.BlockSpec((chans, tile), lambda i: (0, i)),
        ],
        out_specs=pl.BlockSpec((BANDS, shard, tile), lambda i: (0, 0, i)),
        out_shape=jax.ShapeDtypeStruct((BANDS, shard, trials), jnp.float32),
        scratch_shapes=[
            pltpu.VMEM((BANDS, 2, GROUPS, tile), jnp.float32),
            pltpu.VMEM((2, GROUPS, tile), jnp.float32),
            pltpu.VMEM((2, GROUPS, tile), jnp.float32),
            pltpu.VMEM((BANDS, window, tile), jnp.float32),
        ],
        compiler_params=pltpu.CompilerParams(vmem_limit_bytes=60 * 1024 * 1024),
        cost_estimate=pl.CostEstimate(
            flops=2 * pairs * BANDS * 16 * 256 * trials, bytes_accessed=4 << 20, transcendentals=0
        ),
        name="search",
    )(widths, spectra, dm_delay.reshape(chans, trials))


def solution(mesh):
    in_specs = (P("bins", "chan", None), P(), P(), P())
    out_specs = P(None, "bins", "chan")
    return jax.shard_map(shards, mesh=mesh, in_specs=in_specs, out_specs=out_specs, check_vma=False)
```

```python
import math

import jax
import jax.numpy as jnp
import numpy as np
from jax import lax
from jax.experimental import pallas as pl
from jax.experimental.pallas import tpu as pltpu
from jax.sharding import PartitionSpec as P

CHANNELS = 512
GROUPS = 64
BANDS = 8
HALF = 4
FLOOR_VALUE = 0.5
TILE = 512
MESH = pl.DeviceIdType.MESH


def phasor(steps, total):
    shift = (total // 2).bit_length() - 1
    turned = steps + total // 4
    quadrant = turned >> shift
    rest = (turned & (total // 2 - 1)) - total // 4
    x = rest.astype(jnp.float32) * (math.pi / total)
    x2 = x * x
    sine = x + x * x2 * (-1 / 6 + x2 * (1 / 120 + x2 * (-1 / 5040 + x2 * (1 / 362880))))
    cosine = 1.0 + x2 * (-0.5 + x2 * (1 / 24 + x2 * (-1 / 720 + x2 * (1 / 40320))))
    odd = (quadrant & 1) == 1
    c = jnp.where(odd, sine, cosine)
    s = jnp.where(odd, cosine, sine)
    c = jnp.where(((quadrant + 1) & 2) == 2, -c, c)
    s = jnp.where((quadrant & 2) == 2, -s, s)
    return c, s


def times(a, b):
    return a[0] * b[0] - a[1] * b[1], a[0] * b[1] + a[1] * b[0]


def front(phases, chans, shard, samples, groups, table_hbm, out, table, parts, gathered, near, blocks, arrived,
          load_sem, send_sem, recv_sem):
    phase, chan = lax.axis_index("bins"), lax.axis_index("chan")
    window = shard + 2 * HALF
    total = phases * samples.shape[2]
    share = GROUPS // chans
    load = pltpu.make_async_copy(table_hbm, table, load_sem)
    load.start()
    barrier = pltpu.get_barrier_semaphore()
    for off in range(1, chans):
        pl.semaphore_signal(barrier, 1, device_id=(phase, lax.rem(chan + off, chans)), device_id_type=MESH)
    for off in range(1, phases):
        pl.semaphore_signal(barrier, 1, device_id=(lax.rem(phase + off, phases), chan), device_id_type=MESH)

    mine = groups[pl.ds(chan, 1), :]
    chosen = jnp.where(
        mine == lax.broadcasted_iota(jnp.int32, (GROUPS, groups.shape[1]), 0), 1.0, 0.0
    )
    series = jnp.dot(
        chosen, samples[0], precision=lax.Precision.HIGHEST, preferred_element_type=jnp.float32
    )
    parts[...] = series.reshape(parts.shape)
    pl.semaphore_wait(barrier, chans + phases - 2)

    copies = []
    for off in range(1, chans):
        peer = lax.rem(chan + off, chans)
        copy = pltpu.make_async_remote_copy(
            src_ref=parts.at[peer],
            dst_ref=near.at[off - 1],
            send_sem=send_sem.at[off - 1],
            recv_sem=recv_sem.at[off - 1],
            device_id=(phase, peer),
            device_id_type=MESH,
        )
        copy.start()
        copies.append(copy)
    shape = (phases, window, GROUPS)
    place = lax.broadcasted_iota(jnp.int32, shape, 0) * shard + lax.broadcasted_iota(jnp.int32, shape, 1) - HALF
    tc, ts = phasor((2 * phase * place) & (2 * total - 1), total)
    own = parts[chan]
    for copy in copies:
        copy.wait()
    for off in range(1, chans):
        own = own + near[off - 1]
    gathered[pl.ds(chan, 1)] = own[None]

    copies = []
    for off in range(1, chans):
        copy = pltpu.make_async_remote_copy(
            src_ref=gathered.at[chan],
            dst_ref=gathered.at[chan],
            send_sem=send_sem.at[chans - 2 + off],
            recv_sem=recv_sem.at[chans - 2 + off],
            device_id=(phase, lax.rem(chan + off, chans)),
            device_id_type=MESH,
        )
        copy.start()
        copies.append(copy)
    load.wait()
    for copy in copies:
        copy.wait()

    whole = gathered[...].reshape(GROUPS, samples.shape[2])
    high = whole.astype(jnp.bfloat16)
    low = (whole - high.astype(jnp.float32)).astype(jnp.bfloat16)
    dims = (((1,), (1,)), ((), ()))
    freq = (
        lax.dot_general(table[0], high, dims, preferred_element_type=jnp.float32)
        + lax.dot_general(table[0], low, dims, preferred_element_type=jnp.float32)
        + lax.dot_general(table[1], high, dims, preferred_element_type=jnp.float32)
    )
    real = freq[: phases * window].reshape(shape)
    imag = freq[phases * window :].reshape(shape)
    blocks[...] = jnp.concatenate([real * tc + imag * ts, imag * tc - real * ts], axis=2)
    copies = []
    for off in range(1, phases):
        peer = lax.rem(phase + off, phases)
        slot = 2 * (chans - 1) + off - 1
        copy = pltpu.make_async_remote_copy(
            src_ref=blocks.at[peer],
            dst_ref=arrived.at[phase],
            send_sem=send_sem.at[slot],
            recv_sem=recv_sem.at[slot],
            device_id=(peer, chan),
            device_id_type=MESH,
        )
        copy.start()
        copies.append(copy)
    arrived[pl.ds(phase, 1)] = blocks[pl.ds(phase, 1)]
    for copy in copies:
        copy.wait()
    lane = lax.broadcasted_iota(jnp.int32, (window, 2 * GROUPS), 1)
    sign = jnp.where(lane < GROUPS, 1.0, -1.0)
    for band in range(BANDS):
        straight = jnp.zeros((window, 2 * GROUPS), jnp.float32)
        crossed = jnp.zeros((window, 2 * GROUPS), jnp.float32)
        for source in range(phases):
            angle = 2 * math.pi * (source * band % phases) / phases
            block = arrived[source]
            straight += block * math.cos(angle)
            crossed += block * math.sin(angle)
        out[band] = straight + pltpu.roll(crossed, GROUPS, 1) * sign


def search(total, length, shard, widths, spectra, dm, out, centers, offset, step, powers):
    window = shard + 2 * HALF
    pairs = window // 2
    first = lax.axis_index("bins") * shard
    tile = out.shape[2]
    group = lax.broadcasted_iota(jnp.int32, (GROUPS, tile), 0)
    remain = GROUPS - group
    sweep = (2048 * remain * remain) // (GROUPS * GROUPS)
    place = lax.axis_index("chan") * pl.num_programs(0) + pl.program_id(0)
    trial = dm[:, pl.ds(pl.multiple_of(place * tile, tile), tile)]
    delay = (trial * sweep) >> 10
    double = 2 * (first - HALF) + window - 1
    c, s = phasor(delay, total)
    offset[0], offset[1] = c, s
    c, s = phasor(2 * delay, total)
    step[0], step[1] = c, s
    wide = phasor(2 * length * delay, total)
    center = phasor(double * delay, total)
    for band in range(BANDS):
        centers[band, 0], centers[band, 1] = center
        if band < BANDS - 1:
            center = times(center, wide)

    tile8 = (8, 2 * GROUPS)
    row8 = lax.broadcasted_iota(jnp.int32, tile8, 0)
    left = lax.broadcasted_iota(jnp.int32, tile8, 1) < GROUPS
    real_row = (row8 & 1) == 0
    plus_row = (row8 & 2) == 0
    low_part = row8 < 4
    sign_first = jnp.where(real_row & ~left, -1.0, 1.0)
    sign_second = jnp.where(plus_row & (real_row | left) | ~plus_row & ~real_row & ~left, -1.0, 1.0)

    def one_pair(j, carry):
        cb, sb = offset[0], offset[1]
        for duo in range(BANDS // 2):
            row = [
                jnp.broadcast_to(spectra[2 * duo + part, pl.ds(at, 1), :], tile8)
                for part in range(2)
                for at in (pairs + j, pairs - 1 - j)
            ]
            value = jnp.where(
                low_part, jnp.where(plus_row, row[0], row[1]), jnp.where(plus_row, row[2], row[3])
            )
            value = jnp.where(real_row, value, pltpu.roll(value, GROUPS, 1))
            coefs = jnp.concatenate([value * sign_first, value * sign_second], axis=1)
            high = coefs.astype(jnp.bfloat16).astype(jnp.float32)
            rows = jnp.concatenate([high, coefs - high], axis=0).astype(jnp.bfloat16)
            for part in range(2):
                band = 2 * duo + part
                ca, sa = centers[band, 0], centers[band, 1]
                table = jnp.concatenate(
                    [
                        (ca * cb).astype(jnp.bfloat16),
                        (sa * cb).astype(jnp.bfloat16),
                        (sa * sb).astype(jnp.bfloat16),
                        (ca * sb).astype(jnp.bfloat16),
                    ],
                    axis=0,
                )
                both = jnp.dot(rows, table, preferred_element_type=jnp.float32)
                total_rows = both[:8] + both[8:]
                square = total_rows * total_rows * (1.0 / CHANNELS)
                at = 4 * part
                powers[band, pl.ds(pairs + j, 1)] = square[at : at + 1] + square[at + 1 : at + 2]
                powers[band, pl.ds(pairs - 1 - j, 1)] = square[at + 2 : at + 3] + square[at + 3 : at + 4]
        offset[0], offset[1] = times((cb, sb), (step[0], step[1]))
        return carry

    lax.fori_loop(0, pairs, one_pair, 0)

    @pl.when(first == 0)
    def _():
        powers[0, 0:HALF] = jnp.zeros((HALF, tile), jnp.float32)

    @pl.when(first + shard == length)
    def _():
        powers[BANDS - 1, HALF + shard : window] = jnp.zeros((HALF, tile), jnp.float32)

    row = lax.broadcasted_iota(jnp.int32, (shard, 128), 0)
    for band in range(BANDS):
        half_width = widths[band]
        at = row + (band * length + first)
        low_end = jnp.maximum(at - half_width, 0)
        high_end = jnp.minimum(at + half_width, BANDS * length - 1)
        part = 1.0 / (high_end - low_end + 1).astype(jnp.float32)
        weight = [jnp.where(move <= half_width, 1.0, 0.0) for move in range(HALF + 1)]
        for column in range(0, tile, 128):
            lanes = slice(column, column + 128)
            middle = powers[band, HALF : HALF + shard, lanes]
            total_sum = middle
            for move in range(1, HALF + 1):
                total_sum += weight[move] * (
                    powers[band, HALF - move : HALF - move + shard, lanes]
                    + powers[band, HALF + move : HALF + move + shard, lanes]
                )
            out[band, :, lanes] = middle / jnp.maximum(total_sum * part, FLOOR_VALUE)


def block_bins(phases, shard):
    return (np.arange(phases) * shard)[:, None] + np.arange(shard + 2 * HALF)[None, :] - HALF


def spectra_by_kernel(samples, groups, phases, chans, shard):
    local, length = samples.shape[1:]
    window = shard + 2 * HALF
    bins = block_bins(phases, shard)
    turn = ((bins.reshape(-1) % length)[:, None] * np.arange(length)[None, :]) % length
    angle = turn * (2 * np.pi / length)
    scale = (length * phases) ** -0.5
    exact = (np.concatenate([np.cos(angle), -np.sin(angle)], axis=0) * scale).astype(np.float32)
    high = exact.astype(jnp.bfloat16)
    low = (exact - high.astype(np.float32)).astype(jnp.bfloat16)
    table = jnp.asarray(np.stack([high, low]))
    share = GROUPS // chans
    copies = 2 * (chans - 1) + phases - 1
    vmem = pl.BlockSpec(memory_space=pltpu.VMEM)
    return pl.pallas_call(
        lambda *refs: front(phases, chans, shard, *refs),
        in_specs=[vmem, vmem, pl.BlockSpec(memory_space=pl.ANY)],
        out_specs=vmem,
        out_shape=jax.ShapeDtypeStruct((BANDS, window, 2 * GROUPS), jnp.float32),
        scratch_shapes=[
            pltpu.VMEM(table.shape, jnp.bfloat16),
            pltpu.VMEM((chans, share, length), jnp.float32),
            pltpu.VMEM((chans, share, length), jnp.float32),
            pltpu.VMEM((chans - 1, share, length), jnp.float32),
            pltpu.VMEM((phases, window, 2 * GROUPS), jnp.float32),
            pltpu.VMEM((phases, window, 2 * GROUPS), jnp.float32),
            pltpu.SemaphoreType.DMA,
            pltpu.SemaphoreType.DMA((copies,)),
            pltpu.SemaphoreType.DMA((copies,)),
        ],
        compiler_params=pltpu.CompilerParams(
            collective_id=0, has_side_effects=True, vmem_limit_bytes=60 * 1024 * 1024
        ),
        cost_estimate=pl.CostEstimate(flops=1 << 28, bytes_accessed=4 << 20, transcendentals=0),
        name="front",
    )(samples, groups.reshape(chans, local), table)


def spectra_by_collectives(samples, groups, phases, chans, shard):
    highest = lax.Precision.HIGHEST
    phase = lax.axis_index("bins")
    chan = lax.axis_index("chan")
    local, length = samples.shape[1:]
    total = length * phases
    window = shard + 2 * HALF
    share = GROUPS // chans
    mine = lax.dynamic_slice_in_dim(groups, chan * local, local)
    chosen = (mine[None, :] == jnp.arange(GROUPS, dtype=jnp.int32)[:, None]).astype(jnp.float32)
    series = jnp.dot(chosen, samples[0], precision=highest)
    series = lax.psum_scatter(series, "chan", scatter_dimension=0, tiled=True)

    bins = block_bins(phases, shard)
    turn = (np.arange(length)[:, None] * (bins.reshape(-1) % length)[None, :]) % length
    angle = turn * (2 * np.pi / length)
    scale = total**-0.5
    first = np.concatenate([np.cos(angle), -np.sin(angle)], axis=1) * scale
    freq = jnp.dot(series, jnp.asarray(first, jnp.float32), precision=highest)
    freq = freq.reshape(share, 2, phases, window)
    twist = (phase * jnp.asarray(bins, jnp.int32)).astype(jnp.float32) * (2 * math.pi / total)
    tc, ts = jnp.cos(twist), jnp.sin(twist)
    real = freq[:, 0] * tc + freq[:, 1] * ts
    imag = freq[:, 1] * tc - freq[:, 0] * ts
    blocks = jnp.stack([real, imag], axis=0).transpose(2, 0, 1, 3)
    blocks = jnp.broadcast_to(blocks[:, None], (phases, chans, 2, share, window))
    blocks = blocks.reshape(phases * chans, 2, share, window)
    got = lax.all_to_all(blocks, ("bins", "chan"), split_axis=0, concat_axis=0, tiled=True)
    got = got.reshape(phases, chans, 2, share, window)
    second = (np.arange(phases)[:, None] * np.arange(BANDS)[None, :]) % phases * (2 * np.pi / phases)
    c2, s2 = jnp.asarray(np.cos(second), jnp.float32), jnp.asarray(np.sin(second), jnp.float32)
    weave = lambda x, t: jnp.einsum("izgw,ib->bwzg", x, t, precision=highest)
    real = weave(got[:, :, 0], c2) + weave(got[:, :, 1], s2)
    imag = weave(got[:, :, 1], c2) - weave(got[:, :, 0], s2)
    return jnp.stack([real, imag], axis=2).reshape(BANDS, window, 2 * GROUPS)


def shards(samples, groups, dm_delay, widths):
    phases = lax.axis_size("bins")
    chans = lax.axis_size("chan")
    length = samples.shape[2]
    shard = length // phases
    total = length * phases
    window = shard + 2 * HALF
    pairs = window // 2
    make = spectra_by_kernel if window % 8 == 0 else spectra_by_collectives
    spectra = make(samples, groups, phases, chans, shard)
    trials = dm_delay.shape[0] // chans
    tile = min(TILE, trials)
    return pl.pallas_call(
        lambda *refs: search(total, length, shard, *refs),
        grid=(trials // tile,),
        in_specs=[
            pl.BlockSpec(memory_space=pltpu.SMEM),
            pl.BlockSpec(spectra.shape, lambda i: (0, 0, 0)),
            pl.BlockSpec((1, chans * trials), lambda i: (0, 0)),
        ],
        out_specs=pl.BlockSpec((BANDS, shard, tile), lambda i: (0, 0, i)),
        out_shape=jax.ShapeDtypeStruct((BANDS, shard, trials), jnp.float32),
        scratch_shapes=[
            pltpu.VMEM((BANDS, 2, GROUPS, tile), jnp.float32),
            pltpu.VMEM((2, GROUPS, tile), jnp.float32),
            pltpu.VMEM((2, GROUPS, tile), jnp.float32),
            pltpu.VMEM((BANDS, window, tile), jnp.float32),
        ],
        compiler_params=pltpu.CompilerParams(vmem_limit_bytes=60 * 1024 * 1024),
        cost_estimate=pl.CostEstimate(
            flops=2 * pairs * BANDS * 16 * 256 * trials, bytes_accessed=4 << 20, transcendentals=0
        ),
        name="search",
    )(widths, spectra, dm_delay[None])


def solution(mesh):
    in_specs = (P("bins", "chan", None), P(), P(), P())
    out_specs = P(None, "bins", "chan")
    return jax.shard_map(shards, mesh=mesh, in_specs=in_specs, out_specs=out_specs, check_vma=False)
```
